32 devices in a mesh: seq: 16 (over z, y, x), tp: 2 (over core).
Axes of the slice: x: 2, y: 2, z: 4, core: 2. Of those that a mesh axis runs over, the one named last changes fastest.
Arguments:
- student: bfloat16 [4096, 2048], P('seq'), may hold values from -6 to 6
- projector: bfloat16 [2, 4224, 2048], P('tp', 'seq'), may hold values from -0.125 to 0.125
- teacher: bfloat16 [2, 4096, 8448], P(None, 'seq', 'tp'), may hold values from -6 to 6
- layer_index: int32 [4096], P('seq'), may hold values from 0 to 1
- valid_mask: int32 [4096], P('seq'), may hold values 0 or 1
Outputs:
- grad_student: bfloat16 [4096, 2048], P('seq', 'tp')
- token_loss: float32 [4096], P(('seq', 'tp'))
The draws below stay inside these ranges and needn't reach their ends.
All inputs are finite; a program needn't handle non-finite values. No bound on the sum of `valid_mask` on one device may be relied on, other than what follows from the above.
Results may differ from the reference program's by a relative error of at most 0.0034.
Values may be sent and summed in bfloat16 or wider, within the bound.
A program may use at most 64 MiB of HBM per device.

```python
import jax
import jax.numpy as jnp
from jax import lax

D = 2048
HW = 8448
LAYERS = 2
TOK_DEV = 256
TOKENS = 4096
N_SEQ = 16
N_TP = 2


def place_ends(array, key, least, high):
    dims = array.shape
    place = [jax.random.randint(jax.random.fold_in(key, axis), (), 0, dims[axis]) for axis in range(len(dims))]
    array = array.at[tuple(place)].set(least)
    longest = dims.index(max(dims))
    place[longest] = (place[longest] + 1) % dims[longest]
    return array.at[tuple(place)].set(high)


def block_levels(key, dims, split, smallest, largest):
    level, own = 1.0, jax.random.fold_in(key, 6)
    for axis_at, shards_of in split:
        draws = jnp.exp(jax.random.uniform(jax.random.fold_in(own, axis_at), (shards_of,), jnp.float32, smallest / len(split), largest / len(split)))
        level = level * jnp.repeat(draws, dims[axis_at] // shards_of).reshape([-1 if axis == axis_at else 1 for axis in range(len(dims))])
    return level


def noise(rng, dims, deviation, most, shards=(), kind=jnp.bfloat16):
    array = jax.random.normal(rng, dims, jnp.float32) * deviation
    if len(shards) > 0:
        array = block_levels(rng, dims, shards, -0.22, 0.18) * array
    return jnp.clip(array, min=-most, max=most).astype(kind)


def setup_inputs(seed: int = 0) -> dict:
    seeds = jax.random.split(jax.random.key(seed), 6)
    student = noise(seeds[0], (TOKENS, D), 1.0, 6.0, ((0, 16),))
    projector = noise(seeds[1], (N_TP, HW // N_TP, D), D ** -0.5, 0.125, ((0, 2), (1, 16)))
    teacher = noise(seeds[2], (LAYERS, TOKENS, HW), 1.0, 6.0, ((1, 16), (2, 2)))
    layer_index = place_ends(jax.random.randint(seeds[3], (TOKENS,), 0, LAYERS), jax.random.fold_in(seeds[3], 1), 0, LAYERS - 1).astype(jnp.int32)
    valid_mask = place_ends((jax.random.randint(seeds[4], (TOKENS,), 0, 4) < 3).astype(jnp.int32), jax.random.fold_in(seeds[4], 1), 0, 1)
    return dict(student=student, projector=projector, teacher=teacher, layer_index=layer_index, valid_mask=valid_mask)


def reference(student, projector, teacher, layer_index, valid_mask):
    proj_rows = projector.reshape(HW, D)
    chosen = teacher[0]
    for layer in range(1, LAYERS):
        chosen = jnp.where((layer_index == layer)[:, None], teacher[layer], chosen)

    def per_block(operands):
        states, targets, flags = operands
        predicted = jnp.dot(states, proj_rows.T, preferred_element_type=jnp.float32)
        difference = predicted - targets.astype(jnp.float32)
        weight = flags.astype(jnp.float32)[:, None]
        masked_err = (weight * difference).astype(jnp.bfloat16)
        gradient = jnp.dot(masked_err, proj_rows, preferred_element_type=jnp.float32).astype(jnp.bfloat16)
        token_loss = weight[:, 0] * jnp.sum(difference * difference, axis=1) / HW
        return gradient, token_loss

    blocks = (student.reshape(N_SEQ, TOK_DEV, D), chosen.reshape(N_SEQ, TOK_DEV, HW), valid_mask.reshape(N_SEQ, TOK_DEV))
    gradient, token_loss = lax.map(per_block, blocks)
    return gradient.reshape(TOKENS, D), token_loss.reshape(TOKENS)
```

```python
import jax
import jax.numpy as jnp
from jax import lax
from jax.experimental import pallas as pl
from jax.experimental.pallas import tpu as pltpu
from jax.sharding import PartitionSpec as P

MESH = pl.DeviceIdType.MESH
LINE, PLANE, CORES = 4, 4, 2


def plain_body(student, projector, teacher, layer_index, valid_mask):
    rows_dev, feat_dim = student.shape
    chosen = jnp.where((layer_index == 1)[:, None], teacher[1], teacher[0])
    weight = valid_mask.astype(jnp.float32)[:, None]
    gathered = lax.all_gather(projector, "seq", axis=1, tiled=True)
    flat_rows = gathered.reshape(-1, feat_dim)
    predicted = lax.dot_general(
        student, flat_rows, (((1,), (1,)), ((), ())), preferred_element_type=jnp.float32
    )
    difference = predicted - chosen.astype(jnp.float32)
    masked_err = (weight * difference).astype(jnp.bfloat16)
    grad_term = jnp.dot(masked_err, flat_rows, preferred_element_type=jnp.float32)
    squares = jnp.sum(difference * difference, axis=1)
    summed = lax.psum_scatter(grad_term, "tp", scatter_dimension=1, tiled=True)
    totals = lax.psum_scatter(squares, "tp", scatter_dimension=0, tiled=True)
    tp_count = lax.axis_size("tp")
    share_rows = rows_dev // tp_count
    own_mask = lax.dynamic_slice_in_dim(
        valid_mask, lax.axis_index("tp") * share_rows, share_rows
    ).astype(jnp.float32)
    return (summed.astype(jnp.bfloat16), own_mask * totals / (teacher.shape[2] * tp_count))


def kernel(
    student, projector, teacher, layer, mask, grad_out, loss_out,
    held, states, layers, stage, chosen, total, squares, give, take, give_sq, take_sq, done, crossed,
    arrived, up_sem, down_sem, over_sem, own_sem,
    state_send, state_recv, load_sem, ch_send, ch_recv, g_send, g_recv, q_send, q_recv, x_send, x_recv,
):
    feat_dim = student.shape[1]
    half = feat_dim // 2
    rows = projector.shape[1]
    tok = student.shape[0]
    share = tok // CORES
    width = teacher.shape[2] * CORES
    seq, core = lax.axis_index("seq"), lax.axis_index("tp")
    z, q = seq // PLANE, seq % PLANE
    y, x = q // 2, q % 2
    other = 1 - core

    def across(r):
        return (1 - y if r // 2 else y) * 2 + (1 - x if r % 2 else x)

    def device(r, k):
        return (z * PLANE + across(r), k)

    sibling = (seq, other)
    above, below = (seq + PLANE, core), (seq - PLANE, core)

    loads = [pltpu.make_async_copy(teacher, layers, load_sem.at[0])]
    loads[0].start()
    own_state = pltpu.make_async_copy(
        student.at[pl.ds(core * share, share), :], states.at[pl.ds(0, share), :], load_sem.at[1])
    own_state.start()
    own_rows = [
        pltpu.make_async_copy(
            projector.at[0, :, pl.ds(h * half, half)], held.at[h, z, core], own_sem.at[h])
        for h in range(2)
    ]
    for copy in own_rows:
        copy.start()

    barrier = pltpu.get_barrier_semaphore()
    peers = [sibling] + [device(r, k) for r in range(1, PLANE) for k in range(CORES)]
    for peer in peers:
        pl.semaphore_signal(barrier, inc=1, device_id=peer, device_id_type=MESH)

    @pl.when(z > 0)
    def _():
        pl.semaphore_signal(barrier, inc=1, device_id=below, device_id_type=MESH)

    @pl.when(z < LINE - 1)
    def _():
        pl.semaphore_signal(barrier, inc=1, device_id=above, device_id_type=MESH)

    pl.semaphore_wait(barrier, len(peers) + jnp.where(z > 0, 1, 0) + jnp.where(z < LINE - 1, 1, 0))

    def rows_copy(source, h, zs, sem, target):
        return pltpu.make_async_remote_copy(
            src_ref=source, dst_ref=held.at[h, zs, core], send_sem=sem.at[h, zs],
            recv_sem=arrived.at[h, zs, core], device_id=target, device_id_type=MESH)

    def pass_on(source, h, zs, act):
        @pl.when((z < LINE - 1) & (zs <= z))
        def _():
            act(rows_copy(source, h, zs, up_sem, above))

        @pl.when((z > 0) & (zs >= z))
        def _():
            act(rows_copy(source, h, zs, down_sem, below))

        act(rows_copy(source, h, zs, over_sem, sibling))

    def landed(h, zs, k):
        pltpu.make_async_remote_copy(
            src_ref=held.at[h, zs, k], dst_ref=held.at[h, zs, k], send_sem=over_sem.at[h, zs],
            recv_sem=arrived.at[h, zs, k], device_id=sibling, device_id_type=MESH).wait_recv()

    for h in range(2):
        pass_on(projector.at[0, :, pl.ds(h * half, half)], h, z, lambda copy: copy.start())

    state_copies = [
        pltpu.make_async_remote_copy(
            src_ref=student.at[pl.ds(core * share, share), :],
            dst_ref=states.at[pl.ds(r * share, share), :],
            send_sem=state_send.at[r], recv_sem=state_recv.at[r],
            device_id=device(r, core), device_id_type=MESH)
        for r in range(1, PLANE)
    ]
    for copy in state_copies:
        copy.start()

    loads[0].wait()
    step_rows = 32

    def choose(i, carry):
        at = pl.multiple_of(i * step_rows, step_rows)
        second = layer[pl.ds(at, step_rows), :] == 1
        for target in range(PLANE):
            for zs in range(LINE):
                first_column = (zs * PLANE + target) * rows
                base = first_column // 128 * 128
                shift = first_column - base
                span = -(-(shift + rows) // 128) * 128
                a = layers[0, pl.ds(at, step_rows), base:base + span].astype(jnp.float32)
                b = layers[1, pl.ds(at, step_rows), base:base + span].astype(jnp.float32)
                picked = jnp.where(second, b, a)
                if shift:
                    picked = pltpu.roll(picked, span - shift, 1)
                stage[target, zs, pl.ds(at, step_rows), :] = picked[:, :rows].astype(jnp.bfloat16)
        return carry

    lax.fori_loop(0, tok // step_rows, choose, 0)

    def chosen_copy(r, k):
        return pltpu.make_async_remote_copy(
            src_ref=stage.at[across(r), :, pl.ds(k * share, share), :],
            dst_ref=chosen.at[core, :, pl.ds(r * share, share), :],
            send_sem=ch_send.at[r, k], recv_sem=ch_recv.at[r, core],
            device_id=device(r, k), device_id_type=MESH)

    own_chosen = pltpu.make_async_copy(
        stage.at[q, :, pl.ds(core * share, share), :],
        chosen.at[core, :, pl.ds(0, share), :], load_sem.at[2])
    own_chosen.start()
    to_sibling = chosen_copy(0, other)
    to_sibling.start()
    chosen_copies = [chosen_copy(r, k) for r in range(1, PLANE) for k in range(CORES)]
    for copy in chosen_copies:
        copy.start()

    total[...] = jnp.zeros_like(total)
    squares[...] = jnp.zeros_like(squares)

    def arrive(distance):
        for h in range(2):
            for sign in (-1, 1):
                zs = z + sign * distance

                @pl.when((zs >= 0) & (zs < LINE))
                def _():
                    landed(h, zs, core)
                    pass_on(held.at[h, zs, core], h, zs, lambda copy: copy.start())

    arrive(1)
    arrive(2)
    for copy in own_rows:
        copy.wait()
    own_state.wait()
    own_chosen.wait()
    for copy in state_copies:
        copy.wait_recv()
    for r in range(PLANE):
        for k in range(CORES):
            if r == 0:
                continue
            pltpu.make_async_remote_copy(
                src_ref=chosen.at[k, :, pl.ds(r * share, share), :],
                dst_ref=chosen.at[k, :, pl.ds(r * share, share), :],
                send_sem=ch_send.at[r, k], recv_sem=ch_recv.at[r, k],
                device_id=sibling, device_id_type=MESH).wait_recv()
    pltpu.make_async_remote_copy(
        src_ref=chosen.at[other, :, pl.ds(0, share), :],
        dst_ref=chosen.at[other, :, pl.ds(0, share), :],
        send_sem=ch_send.at[0, other], recv_sem=ch_recv.at[0, other],
        device_id=sibling, device_id_type=MESH).wait_recv()

    def work(zs):
        for h in range(2):
            landed(h, zs, other)

        def one(k, carry):
            predicted = sum(
                lax.dot_general(
                    states[:, h * half:(h + 1) * half], held[h, zs, k],
                    (((1,), (1,)), ((), ())), preferred_element_type=jnp.float32)
                for h in range(2))
            difference = predicted - chosen[k, zs].astype(jnp.float32)
            squares[...] += jnp.sum(difference * difference, axis=1, keepdims=True)
            err = difference.astype(jnp.bfloat16)
            for h in range(2):
                total[:, h * half:(h + 1) * half] += jnp.dot(
                    err, held[h, zs, k], preferred_element_type=jnp.float32)
            return carry

        lax.fori_loop(0, CORES, one, 0)

    def round_of(distance, carry):
        @pl.when(distance == LINE - 1)
        def _():
            arrive(LINE - 1)

        @pl.when(z - distance >= 0)
        def _():
            work(z - distance)

        @pl.when((distance > 0) & (z + distance < LINE))
        def _():
            work(z + distance)

        return carry

    lax.fori_loop(0, LINE, round_of, 0)

    def square_row(r):
        column = jnp.broadcast_to(squares[r * share:(r + 1) * share, :], (share, 128))
        return column.T[:8, :]

    sums = []
    for r in (3, 1, 2):
        give[r - 1] = total[r * share:(r + 1) * share, :].astype(jnp.bfloat16)
        copy = pltpu.make_async_remote_copy(
            src_ref=give.at[r - 1], dst_ref=take.at[r - 1],
            send_sem=g_send.at[r - 1], recv_sem=g_recv.at[r - 1],
            device_id=device(r, core), device_id_type=MESH)
        copy.start()
        give_sq[r - 1] = square_row(r)
        copy_sq = pltpu.make_async_remote_copy(
            src_ref=give_sq.at[r - 1], dst_ref=take_sq.at[r - 1],
            send_sem=q_send.at[r - 1], recv_sem=q_recv.at[r - 1],
            device_id=device(r, core), device_id_type=MESH)
        copy_sq.start()
        sums += [copy, copy_sq]
    for copy in sums:
        copy.wait_recv()

    own_weight = mask[pl.ds(pl.multiple_of(core * share, share), share), :].astype(jnp.float32)
    for h in range(2):
        at = slice(h * half, (h + 1) * half)
        summed = total[:share, at]
        for r in range(1, PLANE):
            summed += take[r - 1, :, at].astype(jnp.float32)
        done[h] = (own_weight * summed).astype(jnp.bfloat16)
    cross = pltpu.make_async_remote_copy(
        src_ref=done.at[other], dst_ref=crossed, send_sem=x_send, recv_sem=x_recv,
        device_id=sibling, device_id_type=MESH)
    cross.start()
    grad_out[pl.ds(pl.multiple_of(core * share, share), share), :] = done[core]
    all_squares = square_row(0) + take_sq[0] + take_sq[1] + take_sq[2]
    weight_row = jnp.broadcast_to(own_weight, (share, 128)).T[:8, :]
    loss_out[...] = (weight_row * all_squares / width)[:1, :]
    cross.wait_recv()
    grad_out[pl.ds(pl.multiple_of(other * share, share), share), :] = crossed[...]

    cross.wait_send()
    for copy in sums + state_copies + chosen_copies + [to_sibling]:
        copy.wait_send()

    def sent(zs, carry):
        for h in range(2):
            pass_on(held.at[h, zs, core], h, zs, lambda copy: copy.wait_send())
        return carry

    lax.fori_loop(0, LINE, sent, 0)


def fast_body(student, projector, teacher, layer_index, valid_mask):
    tok, feat_dim = student.shape
    rows = projector.shape[1]
    half, share = feat_dim // 2, tok // CORES
    bf16, f32 = jnp.bfloat16, jnp.float32
    dma = pltpu.SemaphoreType.DMA
    flops = 4 * tok * CORES * rows * LINE * CORES * feat_dim
    grad, loss = pl.pallas_call(
        kernel,
        out_shape=(
            jax.ShapeDtypeStruct((tok, half), bf16),
            jax.ShapeDtypeStruct((1, share), f32),
        ),
        in_specs=[pl.BlockSpec(memory_space=pl.ANY)] * 3
        + [pl.BlockSpec(memory_space=pltpu.VMEM)] * 2,
        out_specs=(pl.BlockSpec(memory_space=pltpu.VMEM),) * 2,
        scratch_shapes=[
            pltpu.VMEM((2, LINE, CORES, rows, half), bf16),
            pltpu.VMEM((PLANE * share, feat_dim), bf16),
            pltpu.VMEM(teacher.shape, bf16),
            pltpu.VMEM((PLANE, LINE, tok, rows), bf16),
            pltpu.VMEM((CORES, LINE, PLANE * share, rows), bf16),
            pltpu.VMEM((PLANE * share, feat_dim), f32),
            pltpu.VMEM((PLANE * share, 1), f32),
            pltpu.VMEM((PLANE - 1, share, feat_dim), bf16),
            pltpu.VMEM((PLANE - 1, share, feat_dim), bf16),
            pltpu.VMEM((PLANE - 1, 8, share), f32),
            pltpu.VMEM((PLANE - 1, 8, share), f32),
            pltpu.VMEM((2, share, half), bf16),
            pltpu.VMEM((share, half), bf16),
            dma((2, LINE, CORES)), dma((2, LINE)), dma((2, LINE)), dma((2, LINE)), dma((2,)),
            dma((PLANE,)), dma((PLANE,)), dma((3,)), dma((PLANE, CORES)), dma((PLANE, CORES)),
            dma((PLANE - 1,)), dma((PLANE - 1,)), dma((PLANE - 1,)), dma((PLANE - 1,)),
            dma(()), dma(()),
        ],
        compiler_params=pltpu.CompilerParams(
            collective_id=0, has_side_effects=True, vmem_limit_bytes=48 * 1024 * 1024),
        cost_estimate=pl.CostEstimate(flops=flops, bytes_accessed=16 * 1024 * 1024, transcendentals=0),
    )(student, projector, teacher, layer_index[:, None], valid_mask[:, None])
    return grad, loss.reshape(share)


def solution(mesh):
    placed = (P("seq", None), P("tp", "seq", None), P(None, "seq", "tp"), P("seq"), P("seq"))
    body = fast_body if dict(mesh.shape) == {"seq": LINE * PLANE, "tp": CORES} else plain_body
    return jax.shard_map(
        body,
        mesh=mesh,
        in_specs=placed,
        out_specs=(P("seq", "tp"), P(("seq", "tp"))),
        check_vma=False,
    )
```

```python
import jax
import jax.numpy as jnp
from jax import lax
from jax.experimental import pallas as pl
from jax.experimental.pallas import tpu as pltpu
from jax.sharding import PartitionSpec as P

MESH = pl.DeviceIdType.MESH
PLACE = {0: 0, 2: 1, 3: 2, 1: 3}
LINE, PLANE, CORES = 4, 4, 2


def plain_body(student, projector, teacher, layer_index, valid_mask):
    rows_dev, feat_dim = student.shape
    chosen = jnp.where((layer_index == 1)[:, None], teacher[1], teacher[0])
    weight = valid_mask.astype(jnp.float32)[:, None]
    gathered = lax.all_gather(projector, "seq", axis=1, tiled=True)
    flat_rows = gathered.reshape(-1, feat_dim)
    predicted = lax.dot_general(
        student, flat_rows, (((1,), (1,)), ((), ())), preferred_element_type=jnp.float32
    )
    difference = predicted - chosen.astype(jnp.float32)
    masked_err = (weight * difference).astype(jnp.bfloat16)
    grad_term = jnp.dot(masked_err, flat_rows, preferred_element_type=jnp.float32)
    squares = jnp.sum(difference * difference, axis=1)
    summed = lax.psum_scatter(grad_term, "tp", scatter_dimension=1, tiled=True)
    totals = lax.psum_scatter(squares, "tp", scatter_dimension=0, tiled=True)
    tp_count = lax.axis_size("tp")
    share_rows = rows_dev // tp_count
    own_mask = lax.dynamic_slice_in_dim(
        valid_mask, lax.axis_index("tp") * share_rows, share_rows
    ).astype(jnp.float32)
    return (summed.astype(jnp.bfloat16), own_mask * totals / (teacher.shape[2] * tp_count))


def kernel(
    student, projector, teacher, layer, mask, grad_out, loss_out,
    held, states, layers, second, stage, chosen, total, squares, errors, give, take, give_mid, take_mid, give_sq, take_sq, done, crossed,
    arrived, up_sem, down_sem, over_sem, own_sem,
    state_send, state_recv, load_sem, ch_send, ch_recv, g_send, g_recv, m_send, m_recv, q_send, q_recv, x_send, x_recv,
):
    feat_dim = student.shape[1]
    half = feat_dim // 2
    rows = projector.shape[1]
    tok = student.shape[0]
    share = tok // CORES
    width = teacher.shape[2] * CORES
    seq, core = lax.axis_index("seq"), lax.axis_index("tp")
    z, q = seq // PLANE, seq % PLANE
    y, x = q // 2, q % 2
    other = 1 - core

    def across(r):
        return (1 - y if r // 2 else y) * 2 + (1 - x if r % 2 else x)

    def device(r, k):
        return (z * PLANE + across(r), k)

    sibling = (seq, other)
    above, below = (seq + PLANE, core), (seq - PLANE, core)

    loads = [pltpu.make_async_copy(teacher, layers, load_sem.at[0])]
    loads[0].start()
    own_state = pltpu.make_async_copy(
        student.at[pl.ds(core * share, share), :], states.at[pl.ds(0, share), :], load_sem.at[1])
    own_state.start()
    own_rows = [
        pltpu.make_async_copy(
            projector.at[0, :, pl.ds(h * half, half)], held.at[h, z, core], own_sem.at[h])
        for h in range(2)
    ]
    for copy in own_rows:
        copy.start()

    barrier = pltpu.get_barrier_semaphore()
    peers = [sibling] + [device(r, k) for r in range(1, PLANE) for k in range(CORES)]
    for peer in peers:
        pl.semaphore_signal(barrier, inc=1, device_id=peer, device_id_type=MESH)

    @pl.when(z > 0)
    def _():
        pl.semaphore_signal(barrier, inc=1, device_id=below, device_id_type=MESH)

    @pl.when(z < LINE - 1)
    def _():
        pl.semaphore_signal(barrier, inc=1, device_id=above, device_id_type=MESH)

    pl.semaphore_wait(barrier, len(peers) + jnp.where(z > 0, 1, 0) + jnp.where(z < LINE - 1, 1, 0))

    def rows_copy(source, h, zs, sem, target):
        return pltpu.make_async_remote_copy(
            src_ref=source, dst_ref=held.at[h, zs, core], send_sem=sem.at[h, zs],
            recv_sem=arrived.at[h, zs, core], device_id=target, device_id_type=MESH)

    def pass_on(source, h, zs, act):
        @pl.when((z < LINE - 1) & (zs <= z))
        def _():
            act(rows_copy(source, h, zs, up_sem, above))

        @pl.when((z > 0) & (zs >= z))
        def _():
            act(rows_copy(source, h, zs, down_sem, below))

        act(rows_copy(source, h, zs, over_sem, sibling))

    def landed(h, zs, k):
        pltpu.make_async_remote_copy(
            src_ref=held.at[h, zs, k], dst_ref=held.at[h, zs, k], send_sem=over_sem.at[h, zs],
            recv_sem=arrived.at[h, zs, k], device_id=sibling, device_id_type=MESH).wait_recv()

    for h in range(2):
        pass_on(projector.at[0, :, pl.ds(h * half, half)], h, z, lambda copy: copy.start())

    state_copies = [
        pltpu.make_async_remote_copy(
            src_ref=student.at[pl.ds(core * share, share), :],
            dst_ref=states.at[pl.ds(PLACE[r] * share, share), :],
            send_sem=state_send.at[r], recv_sem=state_recv.at[r],
            device_id=device(r, core), device_id_type=MESH)
        for r in range(1, PLANE)
    ]
    for copy in state_copies:
        copy.start()

    loads[0].wait()
    step_rows = 32
    for k in range(CORES):
        second[k * share:(k + 1) * share, :] = jnp.broadcast_to(layer[k:k + 1, :], (share, share)).T

    def choose(i, carry):
        at = pl.multiple_of(i * step_rows, step_rows)
        mapped = second[pl.ds(at, step_rows), :1] == 1
        for target in range(PLANE):
            for zs in range(LINE):
                first_column = (zs * PLANE + target) * rows
                base = first_column // 128 * 128
                shift = first_column - base
                span = -(-(shift + rows) // 128) * 128
                a = layers[0, pl.ds(at, step_rows), base:base + span].astype(jnp.float32)
                b = layers[1, pl.ds(at, step_rows), base:base + span].astype(jnp.float32)
                picked = jnp.where(mapped, b, a)
                if shift:
                    picked = pltpu.roll(picked, span - shift, 1)
                stage[target, zs, pl.ds(at, step_rows), :] = picked[:, :rows].astype(jnp.bfloat16)
        return carry

    lax.fori_loop(0, tok // step_rows, choose, 0)

    def chosen_copy(r, k):
        return pltpu.make_async_remote_copy(
            src_ref=stage.at[across(r), :, pl.ds(k * share, share), :],
            dst_ref=chosen.at[core, :, pl.ds(PLACE[r] * share, share), :],
            send_sem=ch_send.at[r, k], recv_sem=ch_recv.at[r, core],
            device_id=device(r, k), device_id_type=MESH)

    own_chosen = pltpu.make_async_copy(
        stage.at[q, :, pl.ds(core * share, share), :],
        chosen.at[core, :, pl.ds(0, share), :], load_sem.at[2])
    own_chosen.start()
    to_sibling = chosen_copy(0, other)
    to_sibling.start()
    chosen_copies = [chosen_copy(r, k) for r in range(1, PLANE) for k in range(CORES)]
    for copy in chosen_copies:
        copy.start()

    total[...] = jnp.zeros_like(total)
    squares[...] = jnp.zeros_like(squares)

    def arrive(distance):
        for h in range(2):
            for sign in (-1, 1):
                zs = z + sign * distance

                @pl.when((zs >= 0) & (zs < LINE))
                def _():
                    landed(h, zs, core)
                    pass_on(held.at[h, zs, core], h, zs, lambda copy: copy.start())

    arrive(1)
    arrive(2)
    for copy in own_rows:
        copy.wait()
    own_state.wait()
    own_chosen.wait()
    for copy in state_copies:
        copy.wait_recv()
    for r in range(PLANE):
        for k in range(CORES):
            if r == 0:
                continue
            pltpu.make_async_remote_copy(
                src_ref=chosen.at[k, :, pl.ds(PLACE[r] * share, share), :],
                dst_ref=chosen.at[k, :, pl.ds(PLACE[r] * share, share), :],
                send_sem=ch_send.at[r, k], recv_sem=ch_recv.at[r, k],
                device_id=sibling, device_id_type=MESH).wait_recv()
    pltpu.make_async_remote_copy(
        src_ref=chosen.at[other, :, pl.ds(0, share), :],
        dst_ref=chosen.at[other, :, pl.ds(0, share), :],
        send_sem=ch_send.at[0, other], recv_sem=ch_recv.at[0, other],
        device_id=sibling, device_id_type=MESH).wait_recv()

    def error_of(zs, k):
        predicted = sum(
            lax.dot_general(
                states[:, h * half:(h + 1) * half], held[h, zs, k],
                (((1,), (1,)), ((), ())), preferred_element_type=jnp.float32)
            for h in range(2))
        difference = predicted - chosen[k, zs].astype(jnp.float32)
        squares[...] += jnp.sum(difference * difference, axis=1, keepdims=True)
        return difference.astype(jnp.bfloat16)

    def work(zs):
        for h in range(2):
            landed(h, zs, other)

        def one(k, carry):
            err = error_of(zs, k)
            for h in range(2):
                total[:, h * half:(h + 1) * half] += jnp.dot(
                    err, held[h, zs, k], preferred_element_type=jnp.float32)
            return carry

        lax.fori_loop(0, CORES, one, 0)

    last = jnp.where(z < LINE // 2, LINE - 1, 0)

    def round_of(distance, carry):
        @pl.when((z - distance >= 0) & (z - distance != last))
        def _():
            work(z - distance)

        @pl.when((distance > 0) & (z + distance < LINE) & (z + distance != last))
        def _():
            work(z + distance)

        return carry

    lax.fori_loop(0, LINE - 1, round_of, 0)
    arrive(LINE - 1)

    errors[0] = error_of(last, core)
    for h in range(2):
        landed(h, last, other)
    errors[1] = error_of(last, other)

    def finish(first, count, h):
        at = slice(first * share, (first + count) * share)
        value = total[at, h * half:(h + 1) * half]
        for i, k in enumerate((core, other)):
            value += jnp.dot(errors[i, at, :], held[h, last, k], preferred_element_type=jnp.float32)
        return value

    sums = []

    def send(source, dest, send_sem, recv_sem, target):
        copy = pltpu.make_async_remote_copy(
            src_ref=source, dst_ref=dest, send_sem=send_sem, recv_sem=recv_sem,
            device_id=target, device_id_type=MESH)
        copy.start()
        sums.append(copy)
        return copy

    def send_half(h, part, target):
        at = pl.ds(part * share, share)
        return send(give.at[h, at, :], take.at[h, at, :], g_send.at[h, part], g_recv.at[h, part], target)

    x_side, y_side = device(1, core), device(2, core)
    give[0] = finish(2, 2, 0).astype(jnp.bfloat16)
    x_mid, x_own = send_half(0, 0, x_side), send_half(0, 1, x_side)
    give[1] = finish(1, 2, 1).astype(jnp.bfloat16)
    y_mid, y_own = send_half(1, 1, y_side), send_half(1, 0, y_side)
    low, high = slice(0, half), slice(half, feat_dim)
    total[:2 * share, low] = finish(0, 2, 0)
    total[3 * share:, high] = finish(3, 1, 1)

    def square_row(r):
        at = slice(PLACE[r] * share, (PLACE[r] + 1) * share)
        column = jnp.broadcast_to(squares[at, :], (share, share))
        return column.T[:8, :]

    x_mid.wait_recv()
    give_mid[0] = (total[share:2 * share, low] + take[0, :share, :].astype(jnp.float32)).astype(jnp.bfloat16)
    mids = [send(give_mid.at[0], take_mid.at[0], m_send.at[0], m_recv.at[0], y_side)]
    y_mid.wait_recv()
    give_mid[1] = (total[3 * share:, high] + take[1, share:, :].astype(jnp.float32)).astype(jnp.bfloat16)
    mids.append(send(give_mid.at[1], take_mid.at[1], m_send.at[1], m_recv.at[1], x_side))
    total[:share, high] = finish(0, 1, 1)
    squared = []
    for r in range(1, PLANE):
        give_sq[r - 1] = square_row(r)
        squared.append(send(
            give_sq.at[r - 1], take_sq.at[r - 1], q_send.at[r - 1], q_recv.at[r - 1], device(r, core)))
    x_own.wait_recv()
    y_own.wait_recv()
    own_take = (take.at[0, pl.ds(share, share), :], take.at[1, pl.ds(0, share), :])
    for h, at in enumerate((low, high)):
        total[:share, at] += own_take[h][...].astype(jnp.float32)
    for copy in squared + mids:
        copy.wait_recv()

    weight_row = mask[pl.ds(core, 1), :].astype(jnp.float32)
    weight = jnp.broadcast_to(weight_row, (share, share)).T[:, :1]
    for h, at in enumerate((low, high)):
        summed = total[:share, at] + take_mid[h].astype(jnp.float32)
        done[h] = (weight * summed).astype(jnp.bfloat16)
    cross = pltpu.make_async_remote_copy(
        src_ref=done.at[other], dst_ref=crossed, send_sem=x_send, recv_sem=x_recv,
        device_id=sibling, device_id_type=MESH)
    cross.start()
    grad_out[pl.ds(pl.multiple_of(core * share, share), share), :] = done[core]
    all_squares = square_row(0) + take_sq[0] + take_sq[1] + take_sq[2]
    loss_out[...] = weight_row * all_squares[:1, :] / width
    cross.wait_recv()
    grad_out[pl.ds(pl.multiple_of(other * share, share), share), :] = crossed[...]

    cross.wait_send()
    for copy in sums + state_copies + chosen_copies + [to_sibling]:
        copy.wait_send()

    def sent(zs, carry):
        for h in range(2):
            pass_on(held.at[h, zs, core], h, zs, lambda copy: copy.wait_send())
        return carry

    lax.fori_loop(0, LINE, sent, 0)


def fast_body(student, projector, teacher, layer_index, valid_mask):
    tok, feat_dim = student.shape
    rows = projector.shape[1]
    half, share = feat_dim // 2, tok // CORES
    bf16, f32 = jnp.bfloat16, jnp.float32
    dma = pltpu.SemaphoreType.DMA
    flops = 4 * tok * CORES * rows * LINE * CORES * feat_dim
    grad, loss = pl.pallas_call(
        kernel,
        out_shape=(
            jax.ShapeDtypeStruct((tok, half), bf16),
            jax.ShapeDtypeStruct((1, share), f32),
        ),
        in_specs=[pl.BlockSpec(memory_space=pl.ANY)] * 3
        + [pl.BlockSpec(memory_space=pltpu.VMEM)] * 2,
        out_specs=(pl.BlockSpec(memory_space=pltpu.VMEM),) * 2,
        scratch_shapes=[
            pltpu.VMEM((2, LINE, CORES, rows, half), bf16),
            pltpu.VMEM((PLANE * share, feat_dim), bf16),
            pltpu.VMEM(teacher.shape, bf16),
            pltpu.VMEM((tok, share), jnp.int32),
            pltpu.VMEM((PLANE, LINE, tok, rows), bf16),
            pltpu.VMEM((CORES, LINE, PLANE * share, rows), bf16),
            pltpu.VMEM((PLANE * share, feat_dim), f32),
            pltpu.VMEM((PLANE * share, 1), f32),
            pltpu.VMEM((CORES, PLANE * share, rows), bf16),
            pltpu.VMEM((2, 2 * share, half), bf16),
            pltpu.VMEM((2, 2 * share, half), bf16),
            pltpu.VMEM((2, share, half), bf16),
            pltpu.VMEM((2, share, half), bf16),
            pltpu.VMEM((PLANE - 1, 8, share), f32),
            pltpu.VMEM((PLANE - 1, 8, share), f32),
            pltpu.VMEM((2, share, half), bf16),
            pltpu.VMEM((share, half), bf16),
            dma((2, LINE, CORES)), dma((2, LINE)), dma((2, LINE)), dma((2, LINE)), dma((2,)),
            dma((PLANE,)), dma((PLANE,)), dma((3,)), dma((PLANE, CORES)), dma((PLANE, CORES)),
            dma((2, 2)), dma((2, 2)), dma((2,)), dma((2,)), dma((PLANE - 1,)), dma((PLANE - 1,)),
            dma(()), dma(()),
        ],
        compiler_params=pltpu.CompilerParams(
            collective_id=0, has_side_effects=True, vmem_limit_bytes=60 * 1024 * 1024),
        cost_estimate=pl.CostEstimate(flops=flops, bytes_accessed=16 * 1024 * 1024, transcendentals=0),
    )(student, projector, teacher, layer_index.reshape(CORES, share), valid_mask.reshape(CORES, share))
    return grad, loss.reshape(share)


def solution(mesh):
    placed = (P("seq", None), P("tp", "seq", None), P(None, "seq", "tp"), P("seq"), P("seq"))
    body = fast_body if dict(mesh.shape) == {"seq": LINE * PLANE, "tp": CORES} else plain_body
    return jax.shard_map(
        body,
        mesh=mesh,
        in_specs=placed,
        out_specs=(P("seq", "tp"), P(("seq", "tp"))),
        check_vma=False,
    )
```

```python
import jax
import jax.numpy as jnp
from jax import lax
from jax.experimental import pallas as pl
from jax.experimental.pallas import tpu as pltpu
from jax.sharding import PartitionSpec as P

MESH = pl.DeviceIdType.MESH
PLACE = {0: 0, 2: 1, 3: 2, 1: 3}
LINE, PLANE, CORES = 4, 4, 2


def plain_body(student, projector, teacher, layer_index, valid_mask):
    rows_dev, feat_dim = student.shape
    chosen = jnp.where((layer_index == 1)[:, None], teacher[1], teacher[0])
    weight = valid_mask.astype(jnp.float32)[:, None]
    gathered = lax.all_gather(projector, "seq", axis=1, tiled=True)
    flat_rows = gathered.reshape(-1, feat_dim)
    predicted = lax.dot_general(
        student, flat_rows, (((1,), (1,)), ((), ())), preferred_element_type=jnp.float32
    )
    difference = predicted - chosen.astype(jnp.float32)
    masked_err = (weight * difference).astype(jnp.bfloat16)
    grad_term = jnp.dot(masked_err, flat_rows, preferred_element_type=jnp.float32)
    squares = jnp.sum(difference * difference, axis=1)
    summed = lax.psum_scatter(grad_term, "tp", scatter_dimension=1, tiled=True)
    totals = lax.psum_scatter(squares, "tp", scatter_dimension=0, tiled=True)
    tp_count = lax.axis_size("tp")
    share_rows = rows_dev // tp_count
    own_mask = lax.dynamic_slice_in_dim(
        valid_mask, lax.axis_index("tp") * share_rows, share_rows
    ).astype(jnp.float32)
    return (summed.astype(jnp.bfloat16), own_mask * totals / (teacher.shape[2] * tp_count))


def kernel(
    student, projector, teacher, layer, mask, grad_out, loss_out,
    held, states, layers, second, stage, stage_rest, chosen, chosen_rest, total, squares, errors, early, give, take, give_mid, take_mid, give_sq, take_sq, done, crossed,
    arrived, up_sem, down_sem, over_sem, own_sem,
    state_send, state_recv, load_sem, ch_send, ch_recv, rest_send, rest_recv, g_send, g_recv, m_send, m_recv, q_send, q_recv, x_send, x_recv,
):
    feat_dim = student.shape[1]
    half = feat_dim // 2
    rows = projector.shape[1]
    whole = rows // 128 * 128
    rest = rows - whole
    tok = student.shape[0]
    share = tok // CORES
    width = teacher.shape[2] * CORES
    seq, core = lax.axis_index("seq"), lax.axis_index("tp")
    z, q = seq // PLANE, seq % PLANE
    y, x = q // 2, q % 2
    other = 1 - core

    def across(r):
        return (1 - y if r // 2 else y) * 2 + (1 - x if r % 2 else x)

    def device(r, k):
        return (z * PLANE + across(r), k)

    sibling = (seq, other)
    above, below = (seq + PLANE, core), (seq - PLANE, core)

    loads = [pltpu.make_async_copy(teacher, layers, load_sem.at[0])]
    loads[0].start()
    own_state = pltpu.make_async_copy(
        student.at[pl.ds(core * share, share), :], states.at[pl.ds(0, share), :], load_sem.at[1])
    own_state.start()
    own_rows = [
        pltpu.make_async_copy(
            projector.at[0, :, pl.ds(h * half, half)], held.at[h, z, core], own_sem.at[h])
        for h in range(2)
    ]
    for copy in own_rows:
        copy.start()

    barrier = pltpu.get_barrier_semaphore()
    peers = [sibling] + [device(r, k) for r in range(1, PLANE) for k in range(CORES)]
    for peer in peers:
        pl.semaphore_signal(barrier, inc=1, device_id=peer, device_id_type=MESH)

    @pl.when(z > 0)
    def _():
        pl.semaphore_signal(barrier, inc=1, device_id=below, device_id_type=MESH)

    @pl.when(z < LINE - 1)
    def _():
        pl.semaphore_signal(barrier, inc=1, device_id=above, device_id_type=MESH)

    pl.semaphore_wait(barrier, len(peers) + jnp.where(z > 0, 1, 0) + jnp.where(z < LINE - 1, 1, 0))

    def rows_copy(source, h, zs, sem, target):
        return pltpu.make_async_remote_copy(
            src_ref=source, dst_ref=held.at[h, zs, core], send_sem=sem.at[h, zs],
            recv_sem=arrived.at[h, zs, core], device_id=target, device_id_type=MESH)

    def pass_on(source, h, zs, act):
        @pl.when((z < LINE - 1) & (zs <= z))
        def _():
            act(rows_copy(source, h, zs, up_sem, above))

        @pl.when((z > 0) & (zs >= z))
        def _():
            act(rows_copy(source, h, zs, down_sem, below))

        act(rows_copy(source, h, zs, over_sem, sibling))

    def landed(h, zs, k):
        pltpu.make_async_remote_copy(
            src_ref=held.at[h, zs, k], dst_ref=held.at[h, zs, k], send_sem=over_sem.at[h, zs],
            recv_sem=arrived.at[h, zs, k], device_id=sibling, device_id_type=MESH).wait_recv()

    def own_rows_out(h):
        pass_on(projector.at[0, :, pl.ds(h * half, half)], h, z, lambda copy: copy.start())

    own_rows_out(0)

    state_copies = [
        pltpu.make_async_remote_copy(
            src_ref=student.at[pl.ds(core * share, share), :],
            dst_ref=states.at[pl.ds(PLACE[r] * share, share), :],
            send_sem=state_send.at[r], recv_sem=state_recv.at[r],
            device_id=device(r, core), device_id_type=MESH)
        for r in range(1, PLANE)
    ]
    for copy in state_copies:
        copy.start()

    loads[0].wait()
    step_rows = 32
    for k in range(CORES):
        second[k * share:(k + 1) * share, :] = jnp.broadcast_to(layer[k:k + 1, :], (share, share)).T

    def choose(i, carry):
        at = pl.multiple_of(i * step_rows, step_rows)
        mapped = second[pl.ds(at, step_rows), :1] == 1
        for target in range(PLANE):
            rests = []
            for zs in range(LINE):
                first_column = (zs * PLANE + target) * rows
                base = first_column // 128 * 128
                shift = first_column - base
                span = -(-(shift + rows) // 128) * 128
                a = layers[0, pl.ds(at, step_rows), base:base + span].astype(jnp.float32)
                b = layers[1, pl.ds(at, step_rows), base:base + span].astype(jnp.float32)
                picked = jnp.where(mapped, b, a)
                if shift:
                    picked = pltpu.roll(picked, span - shift, 1)
                stage[target, zs, pl.ds(at, step_rows), :] = picked[:, :whole].astype(jnp.bfloat16)
                rests.append(picked[:, whole:rows])
            rests.append(jnp.zeros((step_rows, 128 - LINE * rest), jnp.float32))
            stage_rest[target, pl.ds(at, step_rows), :] = jnp.concatenate(rests, axis=1).astype(jnp.bfloat16)
        return carry

    lax.fori_loop(0, tok // step_rows, choose, 0)
    own_rows_out(1)

    def chosen_copy(r, k):
        mine, theirs = pl.ds(k * share, share), pl.ds(PLACE[r] * share, share)
        return [
            pltpu.make_async_remote_copy(
                src_ref=stage.at[across(r), :, mine, :], dst_ref=chosen.at[core, :, theirs, :],
                send_sem=ch_send.at[r, k], recv_sem=ch_recv.at[r, core],
                device_id=device(r, k), device_id_type=MESH),
            pltpu.make_async_remote_copy(
                src_ref=stage_rest.at[across(r), mine, :], dst_ref=chosen_rest.at[core, theirs, :],
                send_sem=rest_send.at[r, k], recv_sem=rest_recv.at[r, core],
                device_id=device(r, k), device_id_type=MESH),
        ]

    own_chosen = [
        pltpu.make_async_copy(
            stage.at[q, :, pl.ds(core * share, share), :],
            chosen.at[core, :, pl.ds(0, share), :], load_sem.at[2]),
        pltpu.make_async_copy(
            stage_rest.at[q, pl.ds(core * share, share), :],
            chosen_rest.at[core, pl.ds(0, share), :], load_sem.at[3]),
    ]
    chosen_copies = chosen_copy(0, other)
    for r in (3, 1, 2):
        for k in range(CORES):
            chosen_copies += chosen_copy(r, k)
    for copy in own_chosen + chosen_copies:
        copy.start()

    total[...] = jnp.zeros_like(total)
    squares[...] = jnp.zeros_like(squares)

    def arrive(distance, halves=(0, 1)):
        for h in halves:
            for sign in (-1, 1):
                zs = z + sign * distance

                @pl.when((zs >= 0) & (zs < LINE))
                def _():
                    landed(h, zs, core)
                    pass_on(held.at[h, zs, core], h, zs, lambda copy: copy.start())

    arrive(1)
    arrive(2)
    for copy in own_rows:
        copy.wait()
    own_state.wait()
    for copy in own_chosen:
        copy.wait()
    for copy in state_copies:
        copy.wait_recv()

    def chosen_landed(r, k):
        at = pl.ds(PLACE[r] * share, share)
        for buffer, send_sem, recv_sem in (
                (chosen.at[k, :, at, :], ch_send, ch_recv), (chosen_rest.at[k, at, :], rest_send, rest_recv)):
            pltpu.make_async_remote_copy(
                src_ref=buffer, dst_ref=buffer, send_sem=send_sem.at[r, k], recv_sem=recv_sem.at[r, k],
                device_id=sibling, device_id_type=MESH).wait_recv()

    chosen_landed(0, other)
    for r in range(1, PLANE):
        for k in range(CORES):
            chosen_landed(r, k)

    def project(zs, k, h):
        return lax.dot_general(
            states[:, h * half:(h + 1) * half], held[h, zs, k],
            (((1,), (1,)), ((), ())), preferred_element_type=jnp.float32)

    def error_of(zs, k, predicted):
        side = pltpu.roll(chosen_rest[k].astype(jnp.float32), (LINE - zs) * rest + 128 - LINE * rest, 1)
        targets = jnp.concatenate([chosen[k, zs].astype(jnp.float32), side[:, :rest]], axis=1)
        difference = predicted - targets
        squares[...] += jnp.sum(difference * difference, axis=1, keepdims=True)
        return difference.astype(jnp.bfloat16)

    def work(zs):
        for h in range(2):
            landed(h, zs, other)

        def one(k, carry):
            err = error_of(zs, k, project(zs, k, 0) + project(zs, k, 1))
            for h in range(2):
                total[:, h * half:(h + 1) * half] += jnp.dot(
                    err, held[h, zs, k], preferred_element_type=jnp.float32)
            return carry

        lax.fori_loop(0, CORES, one, 0)

    last = jnp.where(z < LINE // 2, LINE - 1, 0)

    def round_of(distance, carry):
        @pl.when((z - distance >= 0) & (z - distance != last))
        def _():
            work(z - distance)

        @pl.when((distance > 0) & (z + distance < LINE) & (z + distance != last))
        def _():
            work(z + distance)

        return carry

    lax.fori_loop(0, LINE - 1, round_of, 0)
    arrive(LINE - 1, (0,))

    early[0] = project(last, core, 0)
    landed(0, last, other)
    early[1] = project(last, other, 0)
    arrive(LINE - 1, (1,))
    errors[0] = error_of(last, core, early[0] + project(last, core, 1))
    landed(1, last, other)
    errors[1] = error_of(last, other, early[1] + project(last, other, 1))

    def finish(first, count, h):
        at = slice(first * share, (first + count) * share)
        value = total[at, h * half:(h + 1) * half]
        for i, k in enumerate((core, other)):
            value += jnp.dot(errors[i, at, :], held[h, last, k], preferred_element_type=jnp.float32)
        return value

    sums = []

    def send(source, dest, send_sem, recv_sem, target):
        copy = pltpu.make_async_remote_copy(
            src_ref=source, dst_ref=dest, send_sem=send_sem, recv_sem=recv_sem,
            device_id=target, device_id_type=MESH)
        copy.start()
        sums.append(copy)
        return copy

    def send_half(h, part, target):
        at = pl.ds(part * share, share)
        return send(give.at[h, at, :], take.at[h, at, :], g_send.at[h, part], g_recv.at[h, part], target)

    x_side, y_side = device(1, core), device(2, core)
    low, high = slice(0, half), slice(half, feat_dim)
    give[0, :share, :] = finish(2, 1, 0).astype(jnp.bfloat16)
    x_mid = send_half(0, 0, x_side)
    give[1, share:, :] = finish(2, 1, 1).astype(jnp.bfloat16)
    y_mid = send_half(1, 1, y_side)
    total[:2 * share, low] = finish(0, 2, 0)
    give[0, share:, :] = finish(3, 1, 0).astype(jnp.bfloat16)
    x_own = send_half(0, 1, x_side)
    give[1, :share, :] = finish(1, 1, 1).astype(jnp.bfloat16)
    y_own = send_half(1, 0, y_side)
    total[3 * share:, high] = finish(3, 1, 1)

    def square_row(r):
        at = slice(PLACE[r] * share, (PLACE[r] + 1) * share)
        column = jnp.broadcast_to(squares[at, :], (share, share))
        return column.T[:8, :]

    x_mid.wait_recv()
    give_mid[0] = (total[share:2 * share, low] + take[0, :share, :].astype(jnp.float32)).astype(jnp.bfloat16)
    mids = [send(give_mid.at[0], take_mid.at[0], m_send.at[0], m_recv.at[0], y_side)]
    y_mid.wait_recv()
    give_mid[1] = (total[3 * share:, high] + take[1, share:, :].astype(jnp.float32)).astype(jnp.bfloat16)
    mids.append(send(give_mid.at[1], take_mid.at[1], m_send.at[1], m_recv.at[1], x_side))
    total[:share, high] = finish(0, 1, 1)
    squared = []
    for r in range(1, PLANE):
        give_sq[r - 1] = square_row(r)
        squared.append(send(
            give_sq.at[r - 1], take_sq.at[r - 1], q_send.at[r - 1], q_recv.at[r - 1], device(r, core)))
    x_own.wait_recv()
    y_own.wait_recv()
    own_take = (take.at[0, pl.ds(share, share), :], take.at[1, pl.ds(0, share), :])
    for h, at in enumerate((low, high)):
        total[:share, at] += own_take[h][...].astype(jnp.float32)
    for copy in squared + mids:
        copy.wait_recv()

    weight_row = mask[pl.ds(core, 1), :].astype(jnp.float32)
    weight = jnp.broadcast_to(weight_row, (share, share)).T[:, :1]
    for h, at in enumerate((low, high)):
        summed = total[:share, at] + take_mid[h].astype(jnp.float32)
        done[h] = (weight * summed).astype(jnp.bfloat16)
    cross = pltpu.make_async_remote_copy(
        src_ref=done.at[other], dst_ref=crossed, send_sem=x_send, recv_sem=x_recv,
        device_id=sibling, device_id_type=MESH)
    cross.start()
    grad_out[pl.ds(pl.multiple_of(core * share, share), share), :] = done[core]
    all_squares = square_row(0) + take_sq[0] + take_sq[1] + take_sq[2]
    loss_out[...] = weight_row * all_squares[:1, :] / width
    cross.wait_recv()
    grad_out[pl.ds(pl.multiple_of(other * share, share), share), :] = crossed[...]

    cross.wait_send()
    for copy in sums + state_copies + chosen_copies:
        copy.wait_send()

    def sent(zs, carry):
        for h in range(2):
            pass_on(held.at[h, zs, core], h, zs, lambda copy: copy.wait_send())
        return carry

    lax.fori_loop(0, LINE, sent, 0)


def fast_body(student, projector, teacher, layer_index, valid_mask):
    tok, feat_dim = student.shape
    rows = projector.shape[1]
    half, share, whole = feat_dim // 2, tok // CORES, rows // 128 * 128
    bf16, f32 = jnp.bfloat16, jnp.float32
    dma = pltpu.SemaphoreType.DMA
    flops = 4 * tok * CORES * rows * LINE * CORES * feat_dim
    grad, loss = pl.pallas_call(
        kernel,
        out_shape=(
            jax.ShapeDtypeStruct((tok, half), bf16),
            jax.ShapeDtypeStruct((1, share), f32),
        ),
        in_specs=[pl.BlockSpec(memory_space=pl.ANY)] * 3
        + [pl.BlockSpec(memory_space=pltpu.VMEM)] * 2,
        out_specs=(pl.BlockSpec(memory_space=pltpu.VMEM),) * 2,
        scratch_shapes=[
            pltpu.VMEM((2, LINE, CORES, rows, half), bf16),
            pltpu.VMEM((PLANE * share, feat_dim), bf16),
            pltpu.VMEM(teacher.shape, bf16),
            pltpu.VMEM((tok, share), jnp.int32),
            pltpu.VMEM((PLANE, LINE, tok, whole), bf16),
            pltpu.VMEM((PLANE, tok, 128), bf16),
            pltpu.VMEM((CORES, LINE, PLANE * share, whole), bf16),
            pltpu.VMEM((CORES, PLANE * share, 128), bf16),
            pltpu.VMEM((PLANE * share, feat_dim), f32),
            pltpu.VMEM((PLANE * share, 1), f32),
            pltpu.VMEM((CORES, PLANE * share, rows), bf16),
            pltpu.VMEM((CORES, PLANE * share, rows), f32),
            pltpu.VMEM((2, 2 * share, half), bf16),
            pltpu.VMEM((2, 2 * share, half), bf16),
            pltpu.VMEM((2, share, half), bf16),
            pltpu.VMEM((2, share, half), bf16),
            pltpu.VMEM((PLANE - 1, 8, share), f32),
            pltpu.VMEM((PLANE - 1, 8, share), f32),
            pltpu.VMEM((2, share, half), bf16),
            pltpu.VMEM((share, half), bf16),
            dma((2, LINE, CORES)), dma((2, LINE)), dma((2, LINE)), dma((2, LINE)), dma((2,)),
            dma((PLANE,)), dma((PLANE,)), dma((4,)), dma((PLANE, CORES)), dma((PLANE, CORES)),
            dma((PLANE, CORES)), dma((PLANE, CORES)),
            dma((2, 2)), dma((2, 2)), dma((2,)), dma((2,)), dma((PLANE - 1,)), dma((PLANE - 1,)),
            dma(()), dma(()),
        ],
        compiler_params=pltpu.CompilerParams(
            collective_id=0, has_side_effects=True, vmem_limit_bytes=60 * 1024 * 1024),
        cost_estimate=pl.CostEstimate(flops=flops, bytes_accessed=16 * 1024 * 1024, transcendentals=0),
    )(student, projector, teacher, layer_index.reshape(CORES, share), valid_mask.reshape(CORES, share))
    return grad, loss.reshape(share)


def solution(mesh):
    placed = (P("seq", None), P("tp", "seq", None), P(None, "seq", "tp"), P("seq"), P("seq"))
    body = fast_body if dict(mesh.shape) == {"seq": LINE * PLANE, "tp": CORES} else plain_body
    return jax.shard_map(
        body,
        mesh=mesh,
        in_specs=placed,
        out_specs=(P("seq", "tp"), P(("seq", "tp"))),
        check_vma=False,
    )
```
